32 devices in a mesh: groups: 2 (over y), afd: 4 (over z), tp: 4 (over x, core).
Axes of the slice: x: 2, y: 2, z: 4, core: 2. Of those that a mesh axis runs over, the one named last changes fastest.
Arguments:
- queries: bfloat16 [16, 64, 128], P(('groups', 'afd'), 'tp'), parts along dimension 0, may hold values from -27 to 27
- cache_keys: bfloat16 [16, 4, 256, 128], P(('groups', 'afd'), 'tp'), parts along dimension 0, may hold values from -4 to 4
- cache_values: bfloat16 [16, 4, 256, 128], P(('groups', 'afd'), 'tp'), parts along dimension 0, may hold values from -6 to 6
- new_keys: bfloat16 [16, 4, 128], P(('groups', 'afd'), 'tp'), parts along dimension 0, may hold values from -4 to 4
- new_values: bfloat16 [16, 4, 128], P(('groups', 'afd'), 'tp'), parts along dimension 0, may hold values from -6 to 6
- cache_lengths: int32 [16], P(('groups', 'afd')), parts along dimension 0, may hold values from 1 to 256, as said below
- moe_in: bfloat16 [384, 4096], P(('groups', 'afd'), 'tp'), parts along dimension 0, may hold values from -6 to 6
- expert_ids: int32 [384, 8], P(('groups', 'afd')), parts along dimension 0, may hold values from 0 to 63, all different within a row; in each aligned block of 48 rows (0 to 47, 48 to 95, ...) at most 9 rows name the same one
- gate_index: int32 [384, 8], P(('groups', 'afd')), parts along dimension 0, may hold values from 0 to 255
- gate_table: float32 [256], replicated, may hold values from 0.05 to 1
- gate_weight: bfloat16 [64, 4096, 768], P('afd', None, 'tp'), may hold values from -0.09375 to 0.09375
- up_weight: bfloat16 [64, 4096, 768], P('afd', None, 'tp'), may hold values from -0.09375 to 0.09375
- down_weight: bfloat16 [64, 768, 4096], P('afd', 'tp'), may hold values from -0.21875 to 0.21875
Outputs:
- attn_out: bfloat16 [16, 64, 128], P(('groups', 'afd'), 'tp'), parts along dimension 0
- moe_out: bfloat16 [384, 4096], P(('groups', 'afd'), 'tp'), parts along dimension 0
The draws below stay inside these ranges and needn't reach their ends.
There are 2 independent parts, one for each index of `groups`. The reference program is written for one: setup_inputs(seed, part) draws one part's arguments, and reference() takes and returns one part's arrays. A program takes and returns all parts, laid end to end along the dimension named above; an argument that names none is the same for every part. Nothing has to cross between parts.
Inputs may be any that keep to these rules, and one draw needn't show every extreme that they name: `expert_ids`: among the 48 tokens of one index of afd, no expert is chosen more than 9 times, and in every draw some expert is chosen exactly 9 times there; each token names 8 different experts. `cache_lengths`: some request has all 256 positions valid.
All inputs are finite; a program needn't handle non-finite values.
Results may differ from the reference program's by a relative error of at most 0.013.
Values may be sent and summed in bfloat16 or wider, within the bound.
A program may use at most 192 MiB of HBM per device.

```python
import math
import jax
import jax.numpy as jnp
import numpy as np
from jax import lax

D = 4096
HEADS = 64
KVH = 4
HD = 128
EXPERTS = 64
FFE = 768
TOPK = 8
TABLE = 256
TOK_DEV = 48
CACHE = 256
CAP = 9
TOKENS = 192
REQS = 8
N_AFD = 4
N_TP = 4


def shared_keys(key):
    return jnp.clip(jax.random.normal(key, (REQS, KVH, HD), jnp.float32), -4.0, 4.0)


def draw_new_keys(key, part):
    base_keys = shared_keys(key)
    return base_keys.astype(jnp.bfloat16)


def draw_cache_keys(key, part):
    key = jax.random.fold_in(key, 5)
    drawn = jnp.clip(jax.random.normal(key, (REQS, KVH, CACHE, HD), jnp.float32), -4.0, 4.0)
    return drawn.astype(jnp.bfloat16)


def draw_queries(key, part):
    key = jax.random.fold_in(key, 7)
    first_key = jax.random.fold_in(key, 0)
    drawn = jnp.clip(jax.random.normal(first_key, (REQS, HEADS, HD), jnp.float32), -4.0, 4.0)
    return drawn.astype(jnp.bfloat16)


def draw_cache_lengths(key, part):
    key = jax.random.fold_in(key, 11)
    first_key, second_key = jax.random.split(key)
    lengths = jax.random.randint(first_key, (REQS,), 1, CACHE + 1)
    filled = jax.random.randint(second_key, (), 0, REQS)
    return lengths.at[filled].set(CACHE).astype(jnp.int32)


def place_ends(values, key, low, top_value):
    longest = values.shape.index(max(values.shape))
    spots = []
    for shift in (0, 1):
        where = [jax.random.randint(jax.random.fold_in(key, axis), (), 0, length) for axis, length in enumerate(values.shape)]
        where[longest] = (where[longest] + shift) % values.shape[longest]
        spots.append(tuple(where))
    return values.at[spots[0]].set(low).at[spots[1]].set(top_value)


def levels(key, shape, cuts, low, high):
    level = 1.0
    for position, parts in cuts:
        heights = jax.random.uniform(jax.random.fold_in(jax.random.fold_in(key, 6), position), (parts,), jnp.float32, low / len(cuts), high / len(cuts))
        level = level * jnp.repeat(jnp.exp(heights), shape[position] // parts).reshape((-1,) + (1,) * (len(shape) - 1 - position))
    return level


def deal_out(own_key, own, number, rows, number_of, top, bound, lean):
    sequence = jax.random.permutation(own_key, number_of)
    crowded, common = load_shares(number_of, rows * top, bound, lean, True), load_shares(number_of, rows * top, bound, lean, False)
    places = jnp.arange(number_of)

    def named(sizes, offset_by):
        used = int((sizes > 0).sum())
        fixed = max(1, used // 4)
        passed = fixed + (places - fixed + offset_by * (used - fixed)) % max(1, number_of - fixed)
        return jnp.zeros((number_of,), jnp.int32).at[sequence[jnp.where(places < fixed, places, passed)]].set(jnp.asarray(sizes, jnp.int32))

    sizes = jnp.where(number % 4 == 0, named(crowded, number // 4), named(common, number - number // 4 - 1))
    mixed = jax.random.permutation(jax.random.fold_in(own, 3), number_of)
    giver, sink = mixed[0:number_of // 2 * 2:2], mixed[1:number_of // 2 * 2:2]
    slack = jnp.minimum(sizes[giver] - 1, bound - sizes[sink]) // 2
    slack = jnp.where((giver == sequence[0]) | (sink == sequence[0]) | (sizes[sink] == 0), 0, jnp.maximum(slack, 0))
    passed = jax.random.randint(jax.random.fold_in(own, 4), (number_of // 2,), 0, 1 << 20) % (slack + 1)
    sizes = sizes.at[giver].add(-passed).at[sink].add(passed)
    labels = jnp.searchsorted(jnp.cumsum(sizes), jnp.arange(rows * top), side="right").astype(jnp.int32)
    table = labels.reshape(top, rows).T
    table = table[jax.random.permutation(jax.random.fold_in(own, 1), rows)]
    offset_by = jax.random.randint(jax.random.fold_in(own, 2), (rows, 1), 0, top)
    return jnp.take_along_axis(table, (jnp.arange(top)[None, :] + offset_by) % top, axis=1)


def load_shares(number_of, total, limit, slope, full):
    weights = [(1 << 20) // math.isqrt(rank ** slope) + 1 for rank in range(1, number_of + 1)]
    largest = limit if full else min(limit, max(-(-total // number_of), total * weights[0] // sum(weights)))
    least = 1 if total - largest >= number_of - 1 else 0
    counts, surplus = [largest] + [least] * (number_of - 1), total - largest - least * (number_of - 1)
    while surplus > 0:
        candidates = [i for i in range(1, number_of) if counts[i] < largest] or [i for i in range(1, number_of) if counts[i] < limit]
        whole, left = sum([weights[i] for i in candidates]), surplus
        for i in candidates:
            addition = min(limit - counts[i], max(1, left * weights[i] // whole), surplus)
            counts[i] = counts[i] + addition
            surplus = surplus - addition
    return np.array(counts)


def gaussian(stream_key, dims, width, most, cuts=(), kind=jnp.bfloat16):
    result = jax.random.normal(stream_key, dims, jnp.float32) * width
    if len(cuts) > 0:
        result = levels(stream_key, dims, cuts, -0.22, 0.18) * result
    return jnp.clip(result, min=-most, max=most).astype(kind)


def setup_inputs(seed: int = 0, part: int = 0) -> dict:
    splits = jax.random.split(jax.random.key(seed), 14)
    part_keys = jax.random.split(jax.random.fold_in(splits[13], part), 14)
    queries = draw_queries(jax.random.fold_in(jax.random.fold_in(splits[13], part), 71), part)
    cache_keys = draw_cache_keys(jax.random.fold_in(jax.random.fold_in(splits[13], part), 71), part)
    cache_values = gaussian(part_keys[2], (REQS, KVH, CACHE, HD), 1.0, 6.0, ((0, 4), (1, 4)))
    new_keys = draw_new_keys(jax.random.fold_in(jax.random.fold_in(splits[13], part), 71), part)
    new_values = gaussian(part_keys[4], (REQS, KVH, HD), 1.0, 6.0, ((0, 4), (1, 4)))
    cache_lengths = draw_cache_lengths(jax.random.fold_in(jax.random.fold_in(splits[13], part), 71), part)
    moe_in = gaussian(part_keys[6], (TOKENS, D), 1.0, 6.0, ((0, 4), (1, 4)))
    expert_ids_keys = jax.random.split(jax.random.fold_in(part_keys[7], 1), TOKENS // TOK_DEV)
    expert_ids_turns = jax.random.permutation(jax.random.fold_in(part_keys[7], 3), TOKENS // TOK_DEV)
    expert_ids = jax.vmap(lambda own, number: deal_out(jax.random.fold_in(part_keys[7], 2), own, number, TOK_DEV, EXPERTS, TOPK, CAP, 2))(expert_ids_keys, expert_ids_turns).reshape((TOKENS, TOPK))
    gate_index = place_ends(jax.random.randint(part_keys[8], (TOKENS, TOPK), 0, TABLE), jax.random.fold_in(part_keys[8], 1), 0, TABLE - 1).astype(jnp.int32)
    gate_table = jnp.clip(jnp.exp(jax.random.uniform(splits[9], (TABLE,), jnp.float32, math.log(0.05), math.log(1.0))), 0.05, 1.0)
    gate_weight = gaussian(splits[10], (EXPERTS, D, FFE), D ** -0.5, 0.09375, ((0, 4), (2, 4)))
    up_weight = gaussian(splits[11], (EXPERTS, D, FFE), D ** -0.5, 0.09375, ((0, 4), (2, 4)))
    down_weight = gaussian(splits[12], (EXPERTS, FFE, D), FFE ** -0.5, 0.21875, ((0, 4), (1, 4)))
    return {"queries": queries, "cache_keys": cache_keys, "cache_values": cache_values, "new_keys": new_keys, "new_values": new_values, "cache_lengths": cache_lengths, "moe_in": moe_in, "expert_ids": expert_ids, "gate_index": gate_index, "gate_table": gate_table, "gate_weight": gate_weight, "up_weight": up_weight, "down_weight": down_weight}


def attend(queries, cache_keys, cache_values, new_keys, new_values, cache_lengths):
    requests, head_count, head_width = queries.shape
    kv_heads = cache_keys.shape[1]
    grouped = queries.reshape(requests, kv_heads, head_count // kv_heads, head_width).astype(jnp.float32)
    score_scale = 1.0 / math.sqrt(head_width)
    scores = jnp.einsum('rkgd,rkld->rkgl', grouped, cache_keys.astype(jnp.float32)) * score_scale
    fresh = jnp.einsum('rkgd,rkd->rkg', grouped, new_keys.astype(jnp.float32)) * score_scale
    positions = jnp.arange(cache_keys.shape[2], dtype=jnp.int32)
    valid = positions[None, None, None, :] < cache_lengths[:, None, None, None]
    masked = jnp.where(valid, scores, -jnp.inf)
    largest = jnp.maximum(lax.optimization_barrier(jnp.max(masked, axis=3)), fresh)
    exp_scores = jnp.where(valid, jnp.exp(masked - largest[..., None]), 0.0)
    fresh_prob = jnp.exp(fresh - largest)
    denominator = lax.optimization_barrier(jnp.sum(exp_scores, axis=3)) + fresh_prob
    weights = (exp_scores / denominator[..., None]).astype(jnp.bfloat16)
    fresh_weight = (fresh_prob / denominator).astype(jnp.bfloat16)
    mixed = jnp.einsum('rkgl,rkld->rkgd', weights.astype(jnp.float32), cache_values.astype(jnp.float32))
    mixed = mixed + fresh_weight.astype(jnp.float32)[..., None] * new_values.astype(jnp.float32)[:, :, None, :]
    return mixed.reshape(requests, head_count, head_width).astype(jnp.bfloat16)

def ranks(choice_ids):
    flat_ids = choice_ids.reshape(-1)
    matches = (flat_ids[:, None] == jnp.arange(EXPERTS, dtype=jnp.int32)[None, :]).astype(jnp.int32)
    earlier = jnp.cumsum(matches, axis=0) - matches
    return lax.optimization_barrier(jnp.sum(earlier * matches, axis=1)).reshape(choice_ids.shape)

def reference(queries, cache_keys, cache_values, new_keys, new_values, cache_lengths, moe_in, expert_ids, gate_index, gate_table, gate_weight, up_weight, down_weight):
    attn_out = attend(queries, cache_keys, cache_values, new_keys, new_values, cache_lengths)
    blocks = expert_ids.reshape(N_AFD, TOK_DEV, TOPK)
    slot_rank = jax.vmap(ranks)(blocks).reshape(TOKENS, TOPK)
    source = (jnp.arange(TOKENS, dtype=jnp.int32) // TOK_DEV)[:, None]
    column = (source * CAP + slot_rank).astype(jnp.int32)
    row_count = N_AFD * CAP
    token_ids = jnp.broadcast_to(jnp.arange(TOKENS, dtype=jnp.int32)[:, None], (TOKENS, TOPK))
    holder = jnp.full((EXPERTS, row_count), TOKENS, jnp.int32)
    holder = holder.at[expert_ids, column].set(token_ids)
    padded = jnp.concatenate([moe_in, jnp.zeros((1, D), moe_in.dtype)], axis=0)
    quarter = FFE // N_TP

    def per_expert(expert):
        inputs = padded[holder[expert]]
        gate_part = jnp.dot(inputs, gate_weight[expert], preferred_element_type=jnp.float32)
        up_part = jnp.dot(inputs, up_weight[expert], preferred_element_type=jnp.float32)
        hidden = (jax.nn.silu(gate_part) * up_part).astype(jnp.bfloat16)
        pieces = jnp.einsum('rjf,jfd->jrd', hidden.reshape(row_count, N_TP, quarter).astype(jnp.float32), down_weight[expert].reshape(N_TP, quarter, D).astype(jnp.float32))
        pieces = lax.optimization_barrier(pieces.astype(jnp.bfloat16)).astype(jnp.float32)
        return lax.optimization_barrier(jnp.sum(pieces, axis=0)).astype(jnp.bfloat16)
    expert_rows = lax.map(per_expert, jnp.arange(EXPERTS, dtype=jnp.int32))
    picked = expert_rows[expert_ids, column].astype(jnp.float32)
    raw_gates = gate_table[gate_index]
    route_weight = raw_gates / lax.optimization_barrier(jnp.sum(raw_gates, axis=1, keepdims=True))
    moe_out = jnp.einsum('tk,tkd->td', route_weight, picked).astype(jnp.bfloat16)
    return (attn_out, moe_out)
```

```python
import math

import jax
import jax.numpy as jnp
from jax import lax
from jax.sharding import PartitionSpec as P

EXPERTS = 64


def attend(queries, cache_keys, cache_values, new_keys, new_values, cache_lengths):
    requests, head_count, head_width = queries.shape
    kv_heads = cache_keys.shape[1]
    grouped = queries.reshape(requests, kv_heads, head_count // kv_heads, head_width)
    score_scale = 1.0 / math.sqrt(head_width)
    scores = (
        jnp.einsum("rkgd,rkld->rkgl", grouped, cache_keys, preferred_element_type=jnp.float32)
        * score_scale
    )
    fresh = (
        jnp.einsum("rkgd,rkd->rkg", grouped, new_keys, preferred_element_type=jnp.float32)
        * score_scale
    )
    positions = jnp.arange(cache_keys.shape[2], dtype=jnp.int32)
    valid = positions[None, None, None, :] < cache_lengths[:, None, None, None]
    masked = jnp.where(valid, scores, -jnp.inf)
    largest = jnp.maximum(jnp.max(masked, axis=3), fresh)
    exp_scores = jnp.where(valid, jnp.exp(masked - largest[..., None]), 0.0)
    fresh_prob = jnp.exp(fresh - largest)
    denominator = jnp.sum(exp_scores, axis=3) + fresh_prob
    weights = (exp_scores / denominator[..., None]).astype(jnp.bfloat16)
    fresh_weight = (fresh_prob / denominator).astype(jnp.bfloat16)
    mixed = jnp.einsum("rkgl,rkld->rkgd", weights, cache_values, preferred_element_type=jnp.float32)
    mixed = (
        mixed
        + fresh_weight.astype(jnp.float32)[..., None]
        * new_values.astype(jnp.float32)[:, :, None, :]
    )
    return mixed.reshape(requests, head_count, head_width).astype(jnp.bfloat16)


def on_device(
    queries,
    cache_keys,
    cache_values,
    new_keys,
    new_values,
    cache_lengths,
    moe_in,
    expert_ids,
    gate_index,
    gate_table,
    gate_weight,
    up_weight,
    down_weight,
):
    attn_out = attend(queries, cache_keys, cache_values, new_keys, new_values, cache_lengths)
    held_experts = gate_weight.shape[0]
    owner = lax.axis_index("afd")
    table_hits = (
        gate_index[..., None] == jnp.arange(gate_table.shape[0], dtype=jnp.int32)[None, None, :]
    ).astype(jnp.float32)
    raw_gates = jnp.sum(table_hits * gate_table[None, None, :], axis=2)
    route_weight = raw_gates / jnp.sum(raw_gates, axis=1, keepdims=True)
    chosen = expert_ids[..., None] == jnp.arange(EXPERTS, dtype=jnp.int32)
    routing = jnp.sum(jnp.where(chosen, route_weight[..., None], 0.0), axis=1)
    all_routing = lax.all_gather(routing, "afd", axis=0, tiled=True)
    held_routing = lax.dynamic_slice_in_dim(all_routing, owner * held_experts, held_experts, axis=1)
    all_rows = lax.all_gather(moe_in, "afd", axis=0, tiled=True)
    all_rows = lax.all_gather(all_rows, "tp", axis=1, tiled=True)
    gate_part = jnp.einsum("te,nef->tnf", all_rows, gate_weight, preferred_element_type=jnp.float32)
    up_part = jnp.einsum("te,nef->tnf", all_rows, up_weight, preferred_element_type=jnp.float32)
    hidden = jax.nn.silu(gate_part) * up_part
    scaled = (hidden * held_routing[:, :, None]).astype(jnp.bfloat16)
    partial_value = jnp.einsum("tnf,nfd->td", scaled, down_weight, preferred_element_type=jnp.float32)
    partial_value = partial_value.astype(jnp.bfloat16)
    summed = lax.psum_scatter(partial_value, "tp", scatter_dimension=1, tiled=True)
    moe_out = lax.psum_scatter(summed, "afd", scatter_dimension=0, tiled=True)
    return (attn_out, moe_out)


def solution(mesh):
    placed = (
        P(("groups", "afd"), "tp", None),
        P(("groups", "afd"), "tp", None, None),
        P(("groups", "afd"), "tp", None, None),
        P(("groups", "afd"), "tp", None),
        P(("groups", "afd"), "tp", None),
        P(("groups", "afd")),
        P(("groups", "afd"), "tp"),
        P(("groups", "afd"), None),
        P(("groups", "afd"), None),
        P(),
        P("afd", None, "tp"),
        P("afd", None, "tp"),
        P("afd", "tp", None),
    )
    return jax.shard_map(
        on_device,
        mesh=mesh,
        in_specs=placed,
        out_specs=(P(("groups", "afd"), "tp", None), P(("groups", "afd"), "tp")),
        check_vma=False,
    )
```

```python
import functools
import math

import jax
import jax.numpy as jnp
from jax import lax
from jax.experimental import pallas as pl
from jax.experimental.pallas import tpu as pltpu
from jax.sharding import PartitionSpec as P

EXPERTS = 64
SLOTS = 4


def attend(queries, cache_keys, cache_values, new_keys, new_values, cache_lengths):
    requests, head_count, head_width = queries.shape
    kv_heads = cache_keys.shape[1]
    grouped = queries.reshape(requests, kv_heads, head_count // kv_heads, head_width)
    score_scale = 1.0 / math.sqrt(head_width)
    scores = (
        jnp.einsum("rkgd,rkld->rkgl", grouped, cache_keys, preferred_element_type=jnp.float32)
        * score_scale
    )
    fresh = (
        jnp.einsum("rkgd,rkd->rkg", grouped, new_keys, preferred_element_type=jnp.float32)
        * score_scale
    )
    positions = jnp.arange(cache_keys.shape[2], dtype=jnp.int32)
    valid = positions[None, None, None, :] < cache_lengths[:, None, None, None]
    masked = jnp.where(valid, scores, -jnp.inf)
    largest = jnp.maximum(jnp.max(masked, axis=3), fresh)
    exp_scores = jnp.where(valid, jnp.exp(masked - largest[..., None]), 0.0)
    fresh_prob = jnp.exp(fresh - largest)
    denominator = jnp.sum(exp_scores, axis=3) + fresh_prob
    weights = (exp_scores / denominator[..., None]).astype(jnp.bfloat16)
    fresh_weight = (fresh_prob / denominator).astype(jnp.bfloat16)
    mixed = jnp.einsum("rkgl,rkld->rkgd", weights, cache_values, preferred_element_type=jnp.float32)
    mixed = (
        mixed
        + fresh_weight.astype(jnp.float32)[..., None]
        * new_values.astype(jnp.float32)[:, :, None, :]
    )
    return mixed.reshape(requests, head_count, head_width).astype(jnp.bfloat16)


def on_device(
    queries,
    cache_keys,
    cache_values,
    new_keys,
    new_values,
    cache_lengths,
    moe_in,
    expert_ids,
    gate_index,
    gate_table,
    gate_weight,
    up_weight,
    down_weight,
):
    attn_out = attend(queries, cache_keys, cache_values, new_keys, new_values, cache_lengths)
    held_experts = gate_weight.shape[0]
    owner = lax.axis_index("afd")
    table_hits = (
        gate_index[..., None] == jnp.arange(gate_table.shape[0], dtype=jnp.int32)[None, None, :]
    ).astype(jnp.float32)
    raw_gates = jnp.sum(table_hits * gate_table[None, None, :], axis=2)
    route_weight = raw_gates / jnp.sum(raw_gates, axis=1, keepdims=True)
    chosen = expert_ids[..., None] == jnp.arange(EXPERTS, dtype=jnp.int32)
    routing = jnp.sum(jnp.where(chosen, route_weight[..., None], 0.0), axis=1)
    all_routing = lax.all_gather(routing, "afd", axis=0, tiled=True)
    held_routing = lax.dynamic_slice_in_dim(all_routing, owner * held_experts, held_experts, axis=1)
    all_rows = lax.all_gather(moe_in, "afd", axis=0, tiled=True)
    all_rows = lax.all_gather(all_rows, "tp", axis=1, tiled=True)
    gate_part = jnp.einsum("te,nef->tnf", all_rows, gate_weight, preferred_element_type=jnp.float32)
    up_part = jnp.einsum("te,nef->tnf", all_rows, up_weight, preferred_element_type=jnp.float32)
    hidden = jax.nn.silu(gate_part) * up_part
    scaled = (hidden * held_routing[:, :, None]).astype(jnp.bfloat16)
    partial_value = jnp.einsum("tnf,nfd->td", scaled, down_weight, preferred_element_type=jnp.float32)
    partial_value = partial_value.astype(jnp.bfloat16)
    summed = lax.psum_scatter(partial_value, "tp", scatter_dimension=1, tiled=True)
    moe_out = lax.psum_scatter(summed, "afd", scatter_dimension=0, tiled=True)
    return (attn_out, moe_out)


def fused_kernel(
    owners,
    queries_ref,
    keys_ref,
    values_ref,
    new_keys_ref,
    new_values_ref,
    lengths_ref,
    rows_ref,
    ids_ref,
    index_ref,
    table_ref,
    gate_hbm,
    up_hbm,
    down_hbm,
    attn_ref,
    moe_ref,
    gate_buf,
    up_buf,
    down_buf,
    all_rows,
    routing,
    hidden,
    part,
    core_got,
    x_got,
    z_got,
    gate_sem,
    up_sem,
    down_sem,
    zg_send,
    zg_recv,
    rt_send,
    rt_recv,
    xg_send,
    xg_recv,
    cg_send,
    cg_recv,
    cs_send,
    cs_recv,
    xs_send,
    xs_recv,
    zs_send,
    zs_recv,
):
    owner = lax.axis_index("afd")
    mine = lax.axis_index("tp")
    core_peer = mine + 1 - 2 * lax.rem(mine, 2)
    x_peer = lax.rem(mine + 2, 4)
    diagonal = lax.rem(core_peer + 2, 4)
    tokens, width = rows_ref.shape
    pairs = gate_hbm.shape[0] // 2
    slots = gate_buf.shape[0]
    ffe = gate_hbm.shape[1]
    everyone = owners * tokens

    def pair_copies(pair, slot):
        experts = pl.ds(pair * 2, 2)
        return (
            pltpu.make_async_copy(gate_hbm.at[experts], gate_buf.at[slot], gate_sem.at[slot]),
            pltpu.make_async_copy(up_hbm.at[experts], up_buf.at[slot], up_sem.at[slot]),
        )

    chunk_order = (diagonal, x_peer, core_peer, mine)

    def down_copy(step):
        columns = pl.ds(pl.multiple_of(chunk_order[step] * width, width), width)
        return pltpu.make_async_copy(
            down_hbm.at[:, :, columns], down_buf.at[step], down_sem.at[step]
        )

    def send(src, dst, send_sem, recv_sem, where):
        return pltpu.make_async_remote_copy(
            src_ref=src,
            dst_ref=dst,
            send_sem=send_sem,
            recv_sem=recv_sem,
            device_id=where,
            device_id_type=pl.DeviceIdType.MESH,
        )

    barrier = pltpu.get_barrier_semaphore()
    hops = sorted(range(1, owners), key=lambda j: min(j, owners - j))
    peers = [{"afd": lax.rem(owner + j, owners)} for j in hops]
    for where in peers + [{"tp": x_peer}, {"tp": core_peer}]:
        pl.semaphore_signal(barrier, inc=1, device_id=where, device_id_type=pl.DeviceIdType.MESH)

    for slot in range(slots):
        for copy in pair_copies(slot, slot):
            copy.start()
    for step in range(4):
        down_copy(step).start()

    table = table_ref[...]
    places = lax.broadcasted_iota(jnp.int32, (tokens, table.shape[1]), 1)
    index = index_ref[...]
    raw = [
        jnp.sum(jnp.where(places == index[:, k : k + 1], table, 0.0), axis=1, keepdims=True)
        for k in range(index.shape[1])
    ]
    total = sum(raw[1:], raw[0])
    lanes = lax.broadcasted_iota(jnp.int32, (tokens, 128), 1)
    ids = ids_ref[...]
    placed = jnp.zeros((tokens, 128), jnp.float32)
    for k in range(index.shape[1]):
        placed = placed + jnp.where(lanes == ids[:, k : k + 1], raw[k] / total, 0.0)
    routing[owner] = placed
    all_rows[mine, owner] = rows_ref[...]

    pl.semaphore_wait(barrier, owners - 1 + 2)

    def z_gather(j, sender, target):
        return send(
            all_rows.at[mine, sender],
            all_rows.at[mine, sender],
            zg_send.at[j],
            zg_recv.at[j],
            {"afd": target},
        )

    def route_gather(j, sender, target):
        return send(
            routing.at[sender], routing.at[sender], rt_send.at[j], rt_recv.at[j], {"afd": target}
        )

    def x_gather(j, source):
        return send(
            all_rows.at[mine, source],
            all_rows.at[mine, source],
            xg_send.at[j],
            xg_recv.at[j],
            {"tp": x_peer},
        )

    def x_landed(j, source):
        return send(
            all_rows.at[x_peer, source],
            all_rows.at[x_peer, source],
            xg_send.at[j],
            xg_recv.at[j],
            {"tp": x_peer},
        )

    def core_gather(group, j, column, source):
        return send(
            all_rows.at[column, source],
            all_rows.at[column, source],
            cg_send.at[group, j],
            cg_recv.at[group, j],
            {"tp": core_peer},
        )

    for j in hops:
        target = lax.rem(owner + j, owners)
        z_gather(j, owner, target).start()
    x_gather(0, owner).start()
    core_gather(0, 0, mine, owner).start()
    for j in hops:
        route_gather(j, owner, lax.rem(owner + j, owners)).start()

    requests, heads, head_width = queries_ref.shape
    score_scale = 1.0 / math.sqrt(head_width)
    for r in range(requests):
        query = queries_ref[r]
        scores = (
            lax.dot_general(
                query, keys_ref[r], (((1,), (1,)), ((), ())), preferred_element_type=jnp.float32
            )
            * score_scale
        )
        new_key = new_keys_ref[pl.ds(r, 1), :].astype(jnp.float32)
        new_value = new_values_ref[pl.ds(r, 1), :].astype(jnp.float32)
        fresh = (
            jnp.sum(query.astype(jnp.float32) * new_key, axis=1, keepdims=True) * score_scale
        )
        positions = lax.broadcasted_iota(jnp.int32, scores.shape, 1)
        valid = positions < lengths_ref[r]
        masked = jnp.where(valid, scores, -jnp.inf)
        largest = jnp.maximum(jnp.max(masked, axis=1, keepdims=True), fresh)
        exp_scores = jnp.where(valid, jnp.exp(masked - largest), 0.0)
        fresh_prob = jnp.exp(fresh - largest)
        denominator = jnp.sum(exp_scores, axis=1, keepdims=True) + fresh_prob
        weights = (exp_scores / denominator).astype(jnp.bfloat16)
        fresh_weight = (fresh_prob / denominator).astype(jnp.bfloat16).astype(jnp.float32)
        mixed = jnp.dot(weights, values_ref[r], preferred_element_type=jnp.float32)
        attn_ref[r] = (mixed + fresh_weight * new_value).astype(jnp.bfloat16)

    order = [0] + hops
    for n, j in enumerate(order):
        source = lax.rem(owner + owners - j, owners)
        if j > 0:
            z_gather(j, source, source).wait_recv()
            x_gather(j, source).start()
            core_gather(0, j, mine, source).start()
        if n > 0:
            before = order[n - 1]
            source = lax.rem(owner + owners - before, owners)
            x_landed(before, source).wait_recv()
            core_gather(1, before, x_peer, source).start()
    last = order[-1]
    source = lax.rem(owner + owners - last, owners)
    x_landed(last, source).wait_recv()
    core_gather(1, last, x_peer, source).start()
    for j in order:
        source = lax.rem(owner + owners - j, owners)
        if j > 0:
            route_gather(j, source, source).wait_recv()
        core_gather(0, j, core_peer, source).wait_recv()
        core_gather(1, j, diagonal, source).wait_recv()
    for j in order:
        source = lax.rem(owner + owners - j, owners)
        if j > 0:
            z_gather(j, owner, source).wait_send()
            route_gather(j, owner, source).wait_send()
        x_gather(j, source).wait_send()
        core_gather(0, j, mine, source).wait_send()
        core_gather(1, j, x_peer, source).wait_send()

    gates = routing[...].reshape(everyone, 128)
    expert_lane = lax.broadcasted_iota(jnp.int32, (everyone, 128), 1)
    unit = lax.broadcasted_iota(jnp.int32, (everyone, 2 * ffe), 1)

    def pair_step(pair, carry):
        slot = lax.rem(pair, slots)
        for copy in pair_copies(pair, slot):
            copy.wait()

        def project(buf):
            out = None
            for t in range(4):
                term = lax.dot_general(
                    all_rows[t].reshape(everyone, width),
                    buf[slot, :, :, t * width : (t + 1) * width].reshape(2 * ffe, width),
                    (((1,), (1,)), ((), ())),
                    preferred_element_type=jnp.float32,
                )
                out = term if out is None else out + term
            return out

        gate_part = project(gate_buf)
        up_part = project(up_buf)
        expert = owner * (2 * pairs) + 2 * pair
        first = jnp.sum(jnp.where(expert_lane == expert, gates, 0.0), axis=1, keepdims=True)
        second = jnp.sum(jnp.where(expert_lane == expert + 1, gates, 0.0), axis=1, keepdims=True)
        scale = jnp.where(unit < ffe, first, second)
        value = gate_part / (1.0 + jnp.exp(-gate_part)) * up_part * scale
        hidden[pair] = value.astype(jnp.bfloat16)

        @pl.when(pair + slots < pairs)
        def _():
            for copy in pair_copies(pair + slots, slot):
                copy.start()

        return carry

    lax.fori_loop(0, pairs, pair_step, 0)

    tile = 256

    def down_step(step):
        down_copy(step).wait()

        def tile_step(n, carry):
            columns = pl.ds(pl.multiple_of(n * tile, tile), tile)
            out = None
            for quad in range(pairs // 2):
                left = jnp.concatenate([hidden[2 * quad], hidden[2 * quad + 1]], axis=1)
                right = down_buf[step, 4 * quad : 4 * quad + 4, :, columns]
                term = jnp.dot(
                    left, right.reshape(4 * ffe, tile), preferred_element_type=jnp.float32
                )
                out = term if out is None else out + term
            part[step, :, :, columns] = out.astype(jnp.bfloat16).reshape(owners, tokens, tile)
            return carry

        lax.fori_loop(0, width // tile, tile_step, 0)

    def core_send(k, step):
        return send(
            part.at[step], core_got.at[k], cs_send.at[k], cs_recv.at[k], {"tp": core_peer}
        )

    def x_send(j, piece):
        return send(
            part.at[1, piece], x_got.at[piece], xs_send.at[j], xs_recv.at[j], {"tp": x_peer}
        )

    def z_send(j, piece):
        return send(
            part.at[3, piece], z_got.at[j], zs_send.at[j], zs_recv.at[j], {"afd": piece}
        )

    def add_in(step, piece, got):
        part[step, piece] = (
            part[step, piece].astype(jnp.float32) + got.astype(jnp.float32)
        ).astype(jnp.bfloat16)

    far_first = hops[::-1] + [0]
    down_step(0)
    core_send(0, 0).start()
    down_step(1)
    core_send(0, 0).wait_recv()
    for j in far_first:
        piece = lax.rem(owner + j, owners)
        add_in(1, piece, core_got[0, piece])
        x_send(j, piece).start()
    down_step(2)
    core_send(1, 2).start()
    down_step(3)
    core_send(1, 2).wait_recv()
    for j in far_first:
        piece = lax.rem(owner + j, owners)
        x_send(j, piece).wait_recv()
        part[3, piece] = (
            part[3, piece].astype(jnp.float32)
            + core_got[1, piece].astype(jnp.float32)
            + x_got[piece].astype(jnp.float32)
        ).astype(jnp.bfloat16)
        if j > 0:
            z_send(j, piece).start()
    result = part[3, owner].astype(jnp.float32)
    for j in hops:
        z_send(j, lax.rem(owner + j, owners)).wait_recv()
        result = result + z_got[j].astype(jnp.float32)
    moe_ref[...] = result.astype(jnp.bfloat16)
    core_send(0, 0).wait_send()
    core_send(1, 2).wait_send()
    for j in far_first:
        piece = lax.rem(owner + j, owners)
        x_send(j, piece).wait_send()
        if j > 0:
            z_send(j, piece).wait_send()


def fused(
    queries,
    cache_keys,
    cache_values,
    new_keys,
    new_values,
    cache_lengths,
    moe_in,
    expert_ids,
    gate_index,
    gate_table,
    gate_weight,
    up_weight,
    down_weight,
):
    owners = lax.axis_size("afd")
    tokens, width = moe_in.shape
    held, ffe, full = down_weight.shape
    requests, _, cached, head_width = cache_keys.shape
    vmem = pl.BlockSpec(memory_space=pltpu.VMEM)
    smem = pl.BlockSpec(memory_space=pltpu.SMEM)
    hbm = pl.BlockSpec(memory_space=pl.ANY)
    slots = min(SLOTS, held // 2)
    dma = pltpu.SemaphoreType.DMA
    bf16 = jnp.bfloat16
    return pl.pallas_call(
        functools.partial(fused_kernel, owners),
        out_shape=(
            jax.ShapeDtypeStruct(queries.shape, bf16),
            jax.ShapeDtypeStruct(moe_in.shape, bf16),
        ),
        in_specs=[vmem] * 5 + [smem] + [vmem] * 4 + [hbm] * 3,
        out_specs=(vmem, vmem),
        scratch_shapes=[
            pltpu.VMEM((slots, 2, ffe, full), bf16),
            pltpu.VMEM((slots, 2, ffe, full), bf16),
            pltpu.VMEM((4, held, ffe, width), bf16),
            pltpu.VMEM((4, owners, tokens, width), bf16),
            pltpu.VMEM((owners, tokens, 128), jnp.float32),
            pltpu.VMEM((held // 2, owners * tokens, 2 * ffe), bf16),
            pltpu.VMEM((4, owners, tokens, width), bf16),
            pltpu.VMEM((2, owners, tokens, width), bf16),
            pltpu.VMEM((owners, tokens, width), bf16),
            pltpu.VMEM((owners, tokens, width), bf16),
            dma((slots,)),
            dma((slots,)),
            dma((4,)),
            dma((owners,)),
            dma((owners,)),
            dma((owners,)),
            dma((owners,)),
            dma((owners,)),
            dma((owners,)),
            dma((2, owners)),
            dma((2, owners)),
            dma((2,)),
            dma((2,)),
            dma((owners,)),
            dma((owners,)),
            dma((owners,)),
            dma((owners,)),
        ],
        compiler_params=pltpu.CompilerParams(
            collective_id=0, has_side_effects=True, vmem_limit_bytes=62 * 1024 * 1024
        ),
        cost_estimate=pl.CostEstimate(
            flops=6 * held * owners * tokens * full * ffe,
            bytes_accessed=6 * held * full * ffe,
            transcendentals=held * owners * tokens * ffe,
        ),
    )(
        queries,
        cache_keys.reshape(requests, cached, head_width),
        cache_values.reshape(requests, cached, head_width),
        new_keys.reshape(requests, head_width),
        new_values.reshape(requests, head_width),
        cache_lengths,
        moe_in,
        expert_ids,
        gate_index,
        gate_table.reshape(1, -1),
        jnp.swapaxes(gate_weight, 1, 2),
        jnp.swapaxes(up_weight, 1, 2),
        down_weight,
    )


def either(*args):
    moe_in, gate_weight = args[6], args[10]
    few_rows = lax.axis_size("afd") * moe_in.shape[0] <= 256
    if few_rows and lax.axis_size("tp") == 4 and gate_weight.shape[0] % 4 == 0:
        return fused(*args)
    return on_device(*args)


def solution(mesh):
    placed = (
        P(("groups", "afd"), "tp", None),
        P(("groups", "afd"), "tp", None, None),
        P(("groups", "afd"), "tp", None, None),
        P(("groups", "afd"), "tp", None),
        P(("groups", "afd"), "tp", None),
        P(("groups", "afd")),
        P(("groups", "afd"), "tp"),
        P(("groups", "afd"), None),
        P(("groups", "afd"), None),
        P(),
        P("afd", None, "tp"),
        P("afd", None, "tp"),
        P("afd", "tp", None),
    )
    return jax.shard_map(
        either,
        mesh=mesh,
        in_specs=placed,
        out_specs=(P(("groups", "afd"), "tp", None), P(("groups", "afd"), "tp")),
        check_vma=False,
    )
```

```python
import functools
import math

import jax
import jax.numpy as jnp
from jax import lax
from jax.experimental import pallas as pl
from jax.experimental.pallas import tpu as pltpu
from jax.sharding import PartitionSpec as P

EXPERTS = 64
SLOTS = 2
GROUP = 4


def attend(queries, cache_keys, cache_values, new_keys, new_values, cache_lengths):
    requests, head_count, head_width = queries.shape
    kv_heads = cache_keys.shape[1]
    grouped = queries.reshape(requests, kv_heads, head_count // kv_heads, head_width)
    score_scale = 1.0 / math.sqrt(head_width)
    scores = (
        jnp.einsum("rkgd,rkld->rkgl", grouped, cache_keys, preferred_element_type=jnp.float32)
        * score_scale
    )
    fresh = (
        jnp.einsum("rkgd,rkd->rkg", grouped, new_keys, preferred_element_type=jnp.float32)
        * score_scale
    )
    positions = jnp.arange(cache_keys.shape[2], dtype=jnp.int32)
    valid = positions[None, None, None, :] < cache_lengths[:, None, None, None]
    masked = jnp.where(valid, scores, -jnp.inf)
    largest = jnp.maximum(jnp.max(masked, axis=3), fresh)
    exp_scores = jnp.where(valid, jnp.exp(masked - largest[..., None]), 0.0)
    fresh_prob = jnp.exp(fresh - largest)
    denominator = jnp.sum(exp_scores, axis=3) + fresh_prob
    weights = (exp_scores / denominator[..., None]).astype(jnp.bfloat16)
    fresh_weight = (fresh_prob / denominator).astype(jnp.bfloat16)
    mixed = jnp.einsum("rkgl,rkld->rkgd", weights, cache_values, preferred_element_type=jnp.float32)
    mixed = (
        mixed
        + fresh_weight.astype(jnp.float32)[..., None]
        * new_values.astype(jnp.float32)[:, :, None, :]
    )
    return mixed.reshape(requests, head_count, head_width).astype(jnp.bfloat16)


def on_device(
    queries,
    cache_keys,
    cache_values,
    new_keys,
    new_values,
    cache_lengths,
    moe_in,
    expert_ids,
    gate_index,
    gate_table,
    gate_weight,
    up_weight,
    down_weight,
):
    attn_out = attend(queries, cache_keys, cache_values, new_keys, new_values, cache_lengths)
    held_experts = gate_weight.shape[0]
    owner = lax.axis_index("afd")
    table_hits = (
        gate_index[..., None] == jnp.arange(gate_table.shape[0], dtype=jnp.int32)[None, None, :]
    ).astype(jnp.float32)
    raw_gates = jnp.sum(table_hits * gate_table[None, None, :], axis=2)
    route_weight = raw_gates / jnp.sum(raw_gates, axis=1, keepdims=True)
    chosen = expert_ids[..., None] == jnp.arange(EXPERTS, dtype=jnp.int32)
    routing = jnp.sum(jnp.where(chosen, route_weight[..., None], 0.0), axis=1)
    all_routing = lax.all_gather(routing, "afd", axis=0, tiled=True)
    held_routing = lax.dynamic_slice_in_dim(all_routing, owner * held_experts, held_experts, axis=1)
    all_rows = lax.all_gather(moe_in, "afd", axis=0, tiled=True)
    all_rows = lax.all_gather(all_rows, "tp", axis=1, tiled=True)
    gate_part = jnp.einsum("te,nef->tnf", all_rows, gate_weight, preferred_element_type=jnp.float32)
    up_part = jnp.einsum("te,nef->tnf", all_rows, up_weight, preferred_element_type=jnp.float32)
    hidden = jax.nn.silu(gate_part) * up_part
    scaled = (hidden * held_routing[:, :, None]).astype(jnp.bfloat16)
    partial_value = jnp.einsum("tnf,nfd->td", scaled, down_weight, preferred_element_type=jnp.float32)
    partial_value = partial_value.astype(jnp.bfloat16)
    summed = lax.psum_scatter(partial_value, "tp", scatter_dimension=1, tiled=True)
    moe_out = lax.psum_scatter(summed, "afd", scatter_dimension=0, tiled=True)
    return (attn_out, moe_out)


def fused_kernel(
    owners,
    queries_ref,
    keys_ref,
    values_ref,
    new_keys_ref,
    new_values_ref,
    lengths_ref,
    rows_ref,
    ids_ref,
    index_ref,
    table_ref,
    gate_hbm,
    up_hbm,
    down_hbm,
    attn_ref,
    moe_ref,
    gate_buf,
    up_buf,
    down_buf,
    all_rows,
    routing,
    hidden,
    part,
    core_got,
    x_got,
    z_got,
    gate_sem,
    up_sem,
    down_sem,
    zg_send,
    zg_recv,
    rt_send,
    rt_recv,
    xg_send,
    xg_recv,
    cg_send,
    cg_recv,
    cs_send,
    cs_recv,
    xs_send,
    xs_recv,
    zs_send,
    zs_recv,
):
    owner = lax.axis_index("afd")
    mine = lax.axis_index("tp")
    core_peer = mine + 1 - 2 * lax.rem(mine, 2)
    x_peer = lax.rem(mine + 2, 4)
    diagonal = lax.rem(core_peer + 2, 4)
    tokens, width = rows_ref.shape
    groups = gate_hbm.shape[0] // GROUP
    slots = gate_buf.shape[0]
    ffe = gate_hbm.shape[1]
    everyone = owners * tokens

    def group_copies(group, slot):
        experts = pl.ds(group * GROUP, GROUP)
        return (
            pltpu.make_async_copy(gate_hbm.at[experts], gate_buf.at[slot], gate_sem.at[slot]),
            pltpu.make_async_copy(up_hbm.at[experts], up_buf.at[slot], up_sem.at[slot]),
        )

    chunk_order = (diagonal, x_peer, core_peer, mine)

    def down_copy(step):
        columns = pl.ds(pl.multiple_of(chunk_order[step] * width, width), width)
        return pltpu.make_async_copy(
            down_hbm.at[:, :, columns], down_buf.at[step], down_sem.at[step]
        )

    def send(src, dst, send_sem, recv_sem, where):
        return pltpu.make_async_remote_copy(
            src_ref=src,
            dst_ref=dst,
            send_sem=send_sem,
            recv_sem=recv_sem,
            device_id=where,
            device_id_type=pl.DeviceIdType.MESH,
        )

    barrier = pltpu.get_barrier_semaphore()
    hops = sorted(range(1, owners), key=lambda j: min(j, owners - j))
    peers = [{"afd": lax.rem(owner + j, owners)} for j in hops]
    for where in peers + [{"tp": x_peer}, {"tp": core_peer}]:
        pl.semaphore_signal(barrier, inc=1, device_id=where, device_id_type=pl.DeviceIdType.MESH)

    for slot in range(slots):
        for copy in group_copies(slot, slot):
            copy.start()
    for step in range(4):
        down_copy(step).start()

    table = table_ref[...]
    places = lax.broadcasted_iota(jnp.int32, (tokens, table.shape[1]), 1)
    index = index_ref[...].T
    raw = [
        jnp.sum(jnp.where(places == index[:, k : k + 1], table, 0.0), axis=1, keepdims=True)
        for k in range(index.shape[1])
    ]
    total = sum(raw[1:], raw[0])
    lanes = lax.broadcasted_iota(jnp.int32, (tokens, 128), 1)
    ids = ids_ref[...].T
    placed = jnp.zeros((tokens, 128), jnp.float32)
    for k in range(index.shape[1]):
        placed = placed + jnp.where(lanes == ids[:, k : k + 1], raw[k] / total, 0.0)
    routing[owner] = placed
    all_rows[mine, owner] = rows_ref[...]

    pl.semaphore_wait(barrier, owners - 1 + 2)

    def z_gather(j, sender, target):
        return send(
            all_rows.at[mine, sender],
            all_rows.at[mine, sender],
            zg_send.at[j],
            zg_recv.at[j],
            {"afd": target},
        )

    def route_gather(j, sender, target):
        return send(
            routing.at[sender], routing.at[sender], rt_send.at[j], rt_recv.at[j], {"afd": target}
        )

    def x_gather(j, source):
        return send(
            all_rows.at[mine, source],
            all_rows.at[mine, source],
            xg_send.at[j],
            xg_recv.at[j],
            {"tp": x_peer},
        )

    def x_landed(j, source):
        return send(
            all_rows.at[x_peer, source],
            all_rows.at[x_peer, source],
            xg_send.at[j],
            xg_recv.at[j],
            {"tp": x_peer},
        )

    def core_gather(group, j, column, source):
        return send(
            all_rows.at[column, source],
            all_rows.at[column, source],
            cg_send.at[group, j],
            cg_recv.at[group, j],
            {"tp": core_peer},
        )

    for j in hops:
        target = lax.rem(owner + j, owners)
        z_gather(j, owner, target).start()
    x_gather(0, owner).start()
    core_gather(0, 0, mine, owner).start()
    for j in hops:
        route_gather(j, owner, lax.rem(owner + j, owners)).start()

    requests, heads, head_width = queries_ref.shape
    score_scale = 1.0 / math.sqrt(head_width)
    for r in range(requests):
        query = queries_ref[r]
        scores = (
            lax.dot_general(
                query, keys_ref[r], (((1,), (1,)), ((), ())), preferred_element_type=jnp.float32
            )
            * score_scale
        )
        new_key = new_keys_ref[pl.ds(r, 1), :].astype(jnp.float32)
        new_value = new_values_ref[pl.ds(r, 1), :].astype(jnp.float32)
        fresh = (
            jnp.sum(query.astype(jnp.float32) * new_key, axis=1, keepdims=True) * score_scale
        )
        positions = lax.broadcasted_iota(jnp.int32, scores.shape, 1)
        valid = positions < lengths_ref[r]
        masked = jnp.where(valid, scores, -jnp.inf)
        largest = jnp.maximum(jnp.max(masked, axis=1, keepdims=True), fresh)
        exp_scores = jnp.where(valid, jnp.exp(masked - largest), 0.0)
        fresh_prob = jnp.exp(fresh - largest)
        denominator = jnp.sum(exp_scores, axis=1, keepdims=True) + fresh_prob
        weights = (exp_scores / denominator).astype(jnp.bfloat16)
        fresh_weight = (fresh_prob / denominator).astype(jnp.bfloat16).astype(jnp.float32)
        mixed = jnp.dot(weights, values_ref[r], preferred_element_type=jnp.float32)
        attn_ref[r] = (mixed + fresh_weight * new_value).astype(jnp.bfloat16)

    order = [0] + hops
    for n, j in enumerate(order):
        source = lax.rem(owner + owners - j, owners)
        if j > 0:
            z_gather(j, source, source).wait_recv()
            x_gather(j, source).start()
            core_gather(0, j, mine, source).start()
        if n > 0:
            before = order[n - 1]
            source = lax.rem(owner + owners - before, owners)
            x_landed(before, source).wait_recv()
            core_gather(1, before, x_peer, source).start()
    last = order[-1]
    source = lax.rem(owner + owners - last, owners)
    x_landed(last, source).wait_recv()
    core_gather(1, last, x_peer, source).start()
    for j in order:
        source = lax.rem(owner + owners - j, owners)
        if j > 0:
            route_gather(j, source, source).wait_recv()
        core_gather(0, j, core_peer, source).wait_recv()
        core_gather(1, j, diagonal, source).wait_recv()
    for j in order:
        source = lax.rem(owner + owners - j, owners)
        if j > 0:
            z_gather(j, owner, source).wait_send()
            route_gather(j, owner, source).wait_send()
        x_gather(j, source).wait_send()
        core_gather(0, j, mine, source).wait_send()
        core_gather(1, j, x_peer, source).wait_send()

    gates = routing[...].reshape(everyone, 128)
    expert_lane = lax.broadcasted_iota(jnp.int32, (everyone, 128), 1)
    unit = lax.broadcasted_iota(jnp.int32, (everyone, GROUP * ffe), 1)

    def group_step(group, carry):
        slot = lax.rem(group, slots)
        for copy in group_copies(group, slot):
            copy.wait()

        def project(buf):
            out = None
            for t in range(4):
                term = lax.dot_general(
                    all_rows[t].reshape(everyone, width),
                    buf[slot, :, :, t * width : (t + 1) * width].reshape(GROUP * ffe, width),
                    (((1,), (1,)), ((), ())),
                    preferred_element_type=jnp.float32,
                )
                out = term if out is None else out + term
            return out

        gate_part = project(gate_buf)
        up_part = project(up_buf)
        expert = GROUP * (owner * groups + group)
        scale = None
        for n in range(GROUP):
            column = jnp.sum(
                jnp.where(expert_lane == expert + n, gates, 0.0), axis=1, keepdims=True
            )
            scale = column if scale is None else jnp.where(unit < n * ffe, scale, column)
        value = gate_part / (1.0 + jnp.exp(-gate_part)) * up_part * scale
        hidden[group] = value.astype(jnp.bfloat16)

        @pl.when(group + slots < groups)
        def _():
            for copy in group_copies(group + slots, slot):
                copy.start()

        return carry

    lax.fori_loop(0, groups, group_step, 0)

    tile = 256

    def down_step(step):
        down_copy(step).wait()

        def tile_step(n, carry):
            columns = pl.ds(pl.multiple_of(n * tile, tile), tile)
            out = None
            for group in range(groups):
                right = down_buf[step, GROUP * group : GROUP * (group + 1), :, columns]
                term = jnp.dot(
                    hidden[group],
                    right.reshape(GROUP * ffe, tile),
                    preferred_element_type=jnp.float32,
                )
                out = term if out is None else out + term
            part[step, :, :, columns] = out.astype(jnp.bfloat16).reshape(owners, tokens, tile)
            return carry

        lax.fori_loop(0, width // tile, tile_step, 0)

    def core_send(k, step):
        return send(
            part.at[step], core_got.at[k], cs_send.at[k], cs_recv.at[k], {"tp": core_peer}
        )

    def x_send(j, piece):
        return send(
            part.at[1, piece], x_got.at[piece], xs_send.at[j], xs_recv.at[j], {"tp": x_peer}
        )

    def z_send(j, piece):
        return send(
            part.at[3, piece], z_got.at[j], zs_send.at[j], zs_recv.at[j], {"afd": piece}
        )

    def add_in(step, piece, got):
        part[step, piece] = (
            part[step, piece].astype(jnp.float32) + got.astype(jnp.float32)
        ).astype(jnp.bfloat16)

    far_first = hops[::-1] + [0]
    down_step(0)
    core_send(0, 0).start()
    down_step(1)
    core_send(0, 0).wait_recv()
    for j in far_first:
        piece = lax.rem(owner + j, owners)
        add_in(1, piece, core_got[0, piece])
        x_send(j, piece).start()
    down_step(2)
    core_send(1, 2).start()
    down_step(3)
    core_send(1, 2).wait_recv()
    for j in far_first:
        piece = lax.rem(owner + j, owners)
        x_send(j, piece).wait_recv()
        part[3, piece] = (
            part[3, piece].astype(jnp.float32)
            + core_got[1, piece].astype(jnp.float32)
            + x_got[piece].astype(jnp.float32)
        ).astype(jnp.bfloat16)
        if j > 0:
            z_send(j, piece).start()
    result = part[3, owner].astype(jnp.float32)
    for j in hops:
        z_send(j, lax.rem(owner + j, owners)).wait_recv()
        result = result + z_got[j].astype(jnp.float32)
    moe_ref[...] = result.astype(jnp.bfloat16)
    core_send(0, 0).wait_send()
    core_send(1, 2).wait_send()
    for j in far_first:
        piece = lax.rem(owner + j, owners)
        x_send(j, piece).wait_send()
        if j > 0:
            z_send(j, piece).wait_send()


def fused(
    queries,
    cache_keys,
    cache_values,
    new_keys,
    new_values,
    cache_lengths,
    moe_in,
    expert_ids,
    gate_index,
    gate_table,
    gate_weight,
    up_weight,
    down_weight,
):
    owners = lax.axis_size("afd")
    tokens, width = moe_in.shape
    held, ffe, full = down_weight.shape
    requests, _, cached, head_width = cache_keys.shape
    vmem = pl.BlockSpec(memory_space=pltpu.VMEM)
    smem = pl.BlockSpec(memory_space=pltpu.SMEM)
    hbm = pl.BlockSpec(memory_space=pl.ANY)
    slots = min(SLOTS, held // GROUP)
    dma = pltpu.SemaphoreType.DMA
    bf16 = jnp.bfloat16
    return pl.pallas_call(
        functools.partial(fused_kernel, owners),
        out_shape=(
            jax.ShapeDtypeStruct(queries.shape, bf16),
            jax.ShapeDtypeStruct(moe_in.shape, bf16),
        ),
        in_specs=[vmem] * 5 + [smem] + [vmem] * 4 + [hbm] * 3,
        out_specs=(vmem, vmem),
        scratch_shapes=[
            pltpu.VMEM((slots, GROUP, ffe, full), bf16),
            pltpu.VMEM((slots, GROUP, ffe, full), bf16),
            pltpu.VMEM((4, held, ffe, width), bf16),
            pltpu.VMEM((4, owners, tokens, width), bf16),
            pltpu.VMEM((owners, tokens, 128), jnp.float32),
            pltpu.VMEM((held // GROUP, owners * tokens, GROUP * ffe), bf16),
            pltpu.VMEM((4, owners, tokens, width), bf16),
            pltpu.VMEM((2, owners, tokens, width), bf16),
            pltpu.VMEM((owners, tokens, width), bf16),
            pltpu.VMEM((owners, tokens, width), bf16),
            dma((slots,)),
            dma((slots,)),
            dma((4,)),
            dma((owners,)),
            dma((owners,)),
            dma((owners,)),
            dma((owners,)),
            dma((owners,)),
            dma((owners,)),
            dma((2, owners)),
            dma((2, owners)),
            dma((2,)),
            dma((2,)),
            dma((owners,)),
            dma((owners,)),
            dma((owners,)),
            dma((owners,)),
        ],
        compiler_params=pltpu.CompilerParams(
            collective_id=0, has_side_effects=True, vmem_limit_bytes=62 * 1024 * 1024
        ),
        cost_estimate=pl.CostEstimate(
            flops=6 * held * owners * tokens * full * ffe,
            bytes_accessed=6 * held * full * ffe,
            transcendentals=held * owners * tokens * ffe,
        ),
    )(
        queries,
        cache_keys.reshape(requests, cached, head_width),
        cache_values.reshape(requests, cached, head_width),
        new_keys.reshape(requests, head_width),
        new_values.reshape(requests, head_width),
        cache_lengths,
        moe_in,
        expert_ids.T,
        gate_index.T,
        gate_table.reshape(1, -1),
        jnp.swapaxes(gate_weight, 1, 2),
        jnp.swapaxes(up_weight, 1, 2),
        down_weight,
    )


def either(*args):
    moe_in, gate_weight = args[6], args[10]
    few_rows = lax.axis_size("afd") * moe_in.shape[0] <= 256
    if few_rows and lax.axis_size("tp") == 4 and gate_weight.shape[0] % GROUP == 0:
        return fused(*args)
    return on_device(*args)


def solution(mesh):
    placed = (
        P(("groups", "afd"), "tp", None),
        P(("groups", "afd"), "tp", None, None),
        P(("groups", "afd"), "tp", None, None),
        P(("groups", "afd"), "tp", None),
        P(("groups", "afd"), "tp", None),
        P(("groups", "afd")),
        P(("groups", "afd"), "tp"),
        P(("groups", "afd"), None),
        P(("groups", "afd"), None),
        P(),
        P("afd", None, "tp"),
        P("afd", None, "tp"),
        P("afd", "tp", None),
    )
    return jax.shard_map(
        either,
        mesh=mesh,
        in_specs=placed,
        out_specs=(P(("groups", "afd"), "tp", None), P(("groups", "afd"), "tp")),
        check_vma=False,
    )
```

```python
import functools
import math

import jax
import jax.numpy as jnp
from jax import lax
from jax.experimental import pallas as pl
from jax.experimental.pallas import tpu as pltpu
from jax.sharding import PartitionSpec as P

EXPERTS = 64
SLOTS = 2
GROUP = 4


def attend(queries, cache_keys, cache_values, new_keys, new_values, cache_lengths):
    requests, head_count, head_width = queries.shape
    kv_heads = cache_keys.shape[1]
    grouped = queries.reshape(requests, kv_heads, head_count // kv_heads, head_width)
    score_scale = 1.0 / math.sqrt(head_width)
    scores = (
        jnp.einsum("rkgd,rkld->rkgl", grouped, cache_keys, preferred_element_type=jnp.float32)
        * score_scale
    )
    fresh = (
        jnp.einsum("rkgd,rkd->rkg", grouped, new_keys, preferred_element_type=jnp.float32)
        * score_scale
    )
    positions = jnp.arange(cache_keys.shape[2], dtype=jnp.int32)
    valid = positions[None, None, None, :] < cache_lengths[:, None, None, None]
    masked = jnp.where(valid, scores, -jnp.inf)
    largest = jnp.maximum(jnp.max(masked, axis=3), fresh)
    exp_scores = jnp.where(valid, jnp.exp(masked - largest[..., None]), 0.0)
    fresh_prob = jnp.exp(fresh - largest)
    denominator = jnp.sum(exp_scores, axis=3) + fresh_prob
    weights = (exp_scores / denominator[..., None]).astype(jnp.bfloat16)
    fresh_weight = (fresh_prob / denominator).astype(jnp.bfloat16)
    mixed = jnp.einsum("rkgl,rkld->rkgd", weights, cache_values, preferred_element_type=jnp.float32)
    mixed = (
        mixed
        + fresh_weight.astype(jnp.float32)[..., None]
        * new_values.astype(jnp.float32)[:, :, None, :]
    )
    return mixed.reshape(requests, head_count, head_width).astype(jnp.bfloat16)


def on_device(
    queries,
    cache_keys,
    cache_values,
    new_keys,
    new_values,
    cache_lengths,
    moe_in,
    expert_ids,
    gate_index,
    gate_table,
    gate_weight,
    up_weight,
    down_weight,
):
    attn_out = attend(queries, cache_keys, cache_values, new_keys, new_values, cache_lengths)
    held_experts = gate_weight.shape[0]
    owner = lax.axis_index("afd")
    table_hits = (
        gate_index[..., None] == jnp.arange(gate_table.shape[0], dtype=jnp.int32)[None, None, :]
    ).astype(jnp.float32)
    raw_gates = jnp.sum(table_hits * gate_table[None, None, :], axis=2)
    route_weight = raw_gates / jnp.sum(raw_gates, axis=1, keepdims=True)
    chosen = expert_ids[..., None] == jnp.arange(EXPERTS, dtype=jnp.int32)
    routing = jnp.sum(jnp.where(chosen, route_weight[..., None], 0.0), axis=1)
    all_routing = lax.all_gather(routing, "afd", axis=0, tiled=True)
    held_routing = lax.dynamic_slice_in_dim(all_routing, owner * held_experts, held_experts, axis=1)
    all_rows = lax.all_gather(moe_in, "afd", axis=0, tiled=True)
    all_rows = lax.all_gather(all_rows, "tp", axis=1, tiled=True)
    gate_part = jnp.einsum("te,nef->tnf", all_rows, gate_weight, preferred_element_type=jnp.float32)
    up_part = jnp.einsum("te,nef->tnf", all_rows, up_weight, preferred_element_type=jnp.float32)
    hidden = jax.nn.silu(gate_part) * up_part
    scaled = (hidden * held_routing[:, :, None]).astype(jnp.bfloat16)
    partial_value = jnp.einsum("tnf,nfd->td", scaled, down_weight, preferred_element_type=jnp.float32)
    partial_value = partial_value.astype(jnp.bfloat16)
    summed = lax.psum_scatter(partial_value, "tp", scatter_dimension=1, tiled=True)
    moe_out = lax.psum_scatter(summed, "afd", scatter_dimension=0, tiled=True)
    return (attn_out, moe_out)


def fused_kernel(
    owners,
    queries_ref,
    keys_ref,
    values_ref,
    new_keys_ref,
    new_values_ref,
    lengths_ref,
    rows_ref,
    ids_ref,
    index_ref,
    table_ref,
    gate_hbm,
    up_hbm,
    down_hbm,
    attn_ref,
    moe_ref,
    gate_buf,
    up_buf,
    down_buf,
    all_rows,
    routing,
    hidden,
    part,
    core_got,
    x_got,
    z_got,
    gate_sem,
    up_sem,
    down_sem,
    zg_send,
    zg_recv,
    rt_send,
    rt_recv,
    xg_send,
    xg_recv,
    cg_send,
    cg_recv,
    cs_send,
    cs_recv,
    xs_send,
    xs_recv,
    zs_send,
    zs_recv,
):
    owner = lax.axis_index("afd")
    mine = lax.axis_index("tp")
    core_peer = mine + 1 - 2 * lax.rem(mine, 2)
    x_peer = lax.rem(mine + 2, 4)
    diagonal = lax.rem(core_peer + 2, 4)
    tokens, width = rows_ref.shape
    groups = gate_hbm.shape[0] // GROUP
    slots = gate_buf.shape[0]
    ffe = gate_hbm.shape[1]
    everyone = owners * tokens

    def group_copies(group, slot):
        experts = pl.ds(group * GROUP, GROUP)
        return (
            pltpu.make_async_copy(gate_hbm.at[experts], gate_buf.at[slot], gate_sem.at[slot]),
            pltpu.make_async_copy(up_hbm.at[experts], up_buf.at[slot], up_sem.at[slot]),
        )

    chunk_order = (diagonal, x_peer, core_peer, mine)

    def down_copy(step):
        columns = pl.ds(pl.multiple_of(chunk_order[step] * width, width), width)
        return pltpu.make_async_copy(
            down_hbm.at[:, :, columns], down_buf.at[step], down_sem.at[step]
        )

    def send(src, dst, send_sem, recv_sem, where):
        return pltpu.make_async_remote_copy(
            src_ref=src,
            dst_ref=dst,
            send_sem=send_sem,
            recv_sem=recv_sem,
            device_id=where,
            device_id_type=pl.DeviceIdType.MESH,
        )

    barrier = pltpu.get_barrier_semaphore()
    hops = sorted(range(1, owners), key=lambda j: min(j, owners - j))
    peers = [{"afd": lax.rem(owner + j, owners)} for j in hops]
    for where in peers + [{"tp": x_peer}, {"tp": core_peer}]:
        pl.semaphore_signal(barrier, inc=1, device_id=where, device_id_type=pl.DeviceIdType.MESH)

    for slot in range(slots):
        for copy in group_copies(slot, slot):
            copy.start()
    for step in range(4):
        down_copy(step).start()

    table = table_ref[...]
    places = lax.broadcasted_iota(jnp.int32, (tokens, table.shape[1]), 1)
    index = index_ref[...].T
    raw = [
        jnp.sum(jnp.where(places == index[:, k : k + 1], table, 0.0), axis=1, keepdims=True)
        for k in range(index.shape[1])
    ]
    total = sum(raw[1:], raw[0])
    lanes = lax.broadcasted_iota(jnp.int32, (tokens, 128), 1)
    ids = ids_ref[...].T
    placed = jnp.zeros((tokens, 128), jnp.float32)
    for k in range(index.shape[1]):
        placed = placed + jnp.where(lanes == ids[:, k : k + 1], raw[k] / total, 0.0)
    routing[owner] = placed
    all_rows[mine, owner] = rows_ref[...]

    pl.semaphore_wait(barrier, owners - 1 + 2)

    def z_gather(j, sender, target):
        return send(
            all_rows.at[mine, sender],
            all_rows.at[mine, sender],
            zg_send.at[j],
            zg_recv.at[j],
            {"afd": target},
        )

    def route_gather(j, sender, target):
        return send(
            routing.at[sender], routing.at[sender], rt_send.at[j], rt_recv.at[j], {"afd": target}
        )

    def x_gather(j, source):
        return send(
            all_rows.at[mine, source],
            all_rows.at[mine, source],
            xg_send.at[j],
            xg_recv.at[j],
            {"tp": x_peer},
        )

    def x_landed(j, source):
        return send(
            all_rows.at[x_peer, source],
            all_rows.at[x_peer, source],
            xg_send.at[j],
            xg_recv.at[j],
            {"tp": x_peer},
        )

    def core_gather(group, j, column, source):
        return send(
            all_rows.at[column, source],
            all_rows.at[column, source],
            cg_send.at[group, j],
            cg_recv.at[group, j],
            {"tp": core_peer},
        )

    for j in hops:
        target = lax.rem(owner + j, owners)
        z_gather(j, owner, target).start()
    x_gather(0, owner).start()
    core_gather(0, 0, mine, owner).start()
    for j in hops:
        route_gather(j, owner, lax.rem(owner + j, owners)).start()

    requests, heads, head_width = queries_ref.shape
    score_scale = 1.0 / math.sqrt(head_width)
    for r in range(requests):
        query = queries_ref[r]
        scores = (
            lax.dot_general(
                query, keys_ref[r], (((1,), (1,)), ((), ())), preferred_element_type=jnp.float32
            )
            * score_scale
        )
        new_key = new_keys_ref[pl.ds(r, 1), :].astype(jnp.float32)
        new_value = new_values_ref[pl.ds(r, 1), :].astype(jnp.float32)
        fresh = (
            jnp.sum(query.astype(jnp.float32) * new_key, axis=1, keepdims=True) * score_scale
        )
        positions = lax.broadcasted_iota(jnp.int32, scores.shape, 1)
        valid = positions < lengths_ref[r]
        masked = jnp.where(valid, scores, -jnp.inf)
        largest = jnp.maximum(jnp.max(masked, axis=1, keepdims=True), fresh)
        exp_scores = jnp.where(valid, jnp.exp(masked - largest), 0.0)
        fresh_prob = jnp.exp(fresh - largest)
        denominator = jnp.sum(exp_scores, axis=1, keepdims=True) + fresh_prob
        weights = (exp_scores / denominator).astype(jnp.bfloat16)
        fresh_weight = (fresh_prob / denominator).astype(jnp.bfloat16).astype(jnp.float32)
        mixed = jnp.dot(weights, values_ref[r], preferred_element_type=jnp.float32)
        attn_ref[r] = (mixed + fresh_weight * new_value).astype(jnp.bfloat16)

    order = [0] + hops
    for n, j in enumerate(order):
        source = lax.rem(owner + owners - j, owners)
        if j > 0:
            z_gather(j, source, source).wait_recv()
            x_gather(j, source).start()
            core_gather(0, j, mine, source).start()
        if n > 0:
            before = order[n - 1]
            source = lax.rem(owner + owners - before, owners)
            x_landed(before, source).wait_recv()
            core_gather(1, before, x_peer, source).start()
    last = order[-1]
    source = lax.rem(owner + owners - last, owners)
    x_landed(last, source).wait_recv()
    core_gather(1, last, x_peer, source).start()
    for j in order:
        source = lax.rem(owner + owners - j, owners)
        if j > 0:
            route_gather(j, source, source).wait_recv()
        core_gather(0, j, core_peer, source).wait_recv()
        core_gather(1, j, diagonal, source).wait_recv()
    gates = routing[...].reshape(everyone, 128)
    expert_lane = lax.broadcasted_iota(jnp.int32, (everyone, 128), 1)
    unit = lax.broadcasted_iota(jnp.int32, (everyone, GROUP * ffe), 1)

    def group_step(group, carry):
        slot = lax.rem(group, slots)
        for copy in group_copies(group, slot):
            copy.wait()

        def project(buf):
            out = None
            for t in range(4):
                term = lax.dot_general(
                    all_rows[t].reshape(everyone, width),
                    buf[slot, :, :, t * width : (t + 1) * width].reshape(GROUP * ffe, width),
                    (((1,), (1,)), ((), ())),
                    preferred_element_type=jnp.float32,
                )
                out = term if out is None else out + term
            return out

        gate_part = project(gate_buf)
        up_part = project(up_buf)
        expert = GROUP * (owner * groups + group)
        scale = None
        for n in range(GROUP):
            column = jnp.sum(
                jnp.where(expert_lane == expert + n, gates, 0.0), axis=1, keepdims=True
            )
            scale = column if scale is None else jnp.where(unit < n * ffe, scale, column)
        value = gate_part / (1.0 + jnp.exp(-gate_part)) * up_part * scale
        hidden[group] = value.astype(jnp.bfloat16)

        @pl.when(group + slots < groups)
        def _():
            for copy in group_copies(group + slots, slot):
                copy.start()

        return carry

    lax.fori_loop(0, groups, group_step, 0)

    tile = 256

    def down_step(step):
        down_copy(step).wait()

        def tile_step(n, carry):
            columns = pl.ds(pl.multiple_of(n * tile, tile), tile)
            out = None
            for group in range(groups):
                right = down_buf[step, GROUP * group : GROUP * (group + 1), :, columns]
                term = jnp.dot(
                    hidden[group],
                    right.reshape(GROUP * ffe, tile),
                    preferred_element_type=jnp.float32,
                )
                out = term if out is None else out + term
            part[step, :, :, columns] = out.astype(jnp.bfloat16).reshape(owners, tokens, tile)
            return carry

        lax.fori_loop(0, width // tile, tile_step, 0)

    def core_send(k, step, j):
        piece = lax.rem(owner + j, owners)
        return send(
            part.at[step, piece],
            core_got.at[k, piece],
            cs_send.at[k, j],
            cs_recv.at[k, j],
            {"tp": core_peer},
        )

    def x_send(j, piece):
        return send(
            part.at[1, piece], x_got.at[piece], xs_send.at[j], xs_recv.at[j], {"tp": x_peer}
        )

    def z_send(j, piece):
        return send(
            part.at[3, piece], z_got.at[j], zs_send.at[j], zs_recv.at[j], {"afd": piece}
        )

    def add_in(step, piece, got):
        part[step, piece] = (
            part[step, piece].astype(jnp.float32) + got.astype(jnp.float32)
        ).astype(jnp.bfloat16)

    far_first = hops[::-1] + [0]
    down_step(0)
    for j in far_first:
        core_send(0, 0, j).start()
    down_step(1)
    for j in far_first:
        piece = lax.rem(owner + j, owners)
        core_send(0, 0, j).wait_recv()
        add_in(1, piece, core_got[0, piece])
        x_send(j, piece).start()
    down_step(2)
    for j in far_first:
        core_send(1, 2, j).start()
    down_step(3)
    for j in far_first:
        piece = lax.rem(owner + j, owners)
        core_send(1, 2, j).wait_recv()
        x_send(j, piece).wait_recv()
        part[3, piece] = (
            part[3, piece].astype(jnp.float32)
            + core_got[1, piece].astype(jnp.float32)
            + x_got[piece].astype(jnp.float32)
        ).astype(jnp.bfloat16)
        if j > 0:
            z_send(j, piece).start()
    result = part[3, owner].astype(jnp.float32)
    for j in hops:
        z_send(j, lax.rem(owner + j, owners)).wait_recv()
        result = result + z_got[j].astype(jnp.float32)
    moe_ref[...] = result.astype(jnp.bfloat16)
    for j in far_first:
        piece = lax.rem(owner + j, owners)
        core_send(0, 0, j).wait_send()
        core_send(1, 2, j).wait_send()
        x_send(j, piece).wait_send()
        if j > 0:
            z_send(j, piece).wait_send()
    for j in order:
        source = lax.rem(owner + owners - j, owners)
        if j > 0:
            z_gather(j, owner, source).wait_send()
            route_gather(j, owner, source).wait_send()
        x_gather(j, source).wait_send()
        core_gather(0, j, mine, source).wait_send()
        core_gather(1, j, x_peer, source).wait_send()


def fused(
    queries,
    cache_keys,
    cache_values,
    new_keys,
    new_values,
    cache_lengths,
    moe_in,
    expert_ids,
    gate_index,
    gate_table,
    gate_weight,
    up_weight,
    down_weight,
):
    owners = lax.axis_size("afd")
    tokens, width = moe_in.shape
    held, ffe, full = down_weight.shape
    requests, _, cached, head_width = cache_keys.shape
    vmem = pl.BlockSpec(memory_space=pltpu.VMEM)
    smem = pl.BlockSpec(memory_space=pltpu.SMEM)
    hbm = pl.BlockSpec(memory_space=pl.ANY)
    slots = min(SLOTS, held // GROUP)
    dma = pltpu.SemaphoreType.DMA
    bf16 = jnp.bfloat16
    return pl.pallas_call(
        functools.partial(fused_kernel, owners),
        out_shape=(
            jax.ShapeDtypeStruct(queries.shape, bf16),
            jax.ShapeDtypeStruct(moe_in.shape, bf16),
        ),
        in_specs=[vmem] * 5 + [smem] + [vmem] * 4 + [hbm] * 3,
        out_specs=(vmem, vmem),
        scratch_shapes=[
            pltpu.VMEM((slots, GROUP, ffe, full), bf16),
            pltpu.VMEM((slots, GROUP, ffe, full), bf16),
            pltpu.VMEM((4, held, ffe, width), bf16),
            pltpu.VMEM((4, owners, tokens, width), bf16),
            pltpu.VMEM((owners, tokens, 128), jnp.float32),
            pltpu.VMEM((held // GROUP, owners * tokens, GROUP * ffe), bf16),
            pltpu.VMEM((4, owners, tokens, width), bf16),
            pltpu.VMEM((2, owners, tokens, width), bf16),
            pltpu.VMEM((owners, tokens, width), bf16),
            pltpu.VMEM((owners, tokens, width), bf16),
            dma((slots,)),
            dma((slots,)),
            dma((4,)),
            dma((owners,)),
            dma((owners,)),
            dma((owners,)),
            dma((owners,)),
            dma((owners,)),
            dma((owners,)),
            dma((2, owners)),
            dma((2, owners)),
            dma((2, owners)),
            dma((2, owners)),
            dma((owners,)),
            dma((owners,)),
            dma((owners,)),
            dma((owners,)),
        ],
        compiler_params=pltpu.CompilerParams(
            collective_id=0, has_side_effects=True, vmem_limit_bytes=62 * 1024 * 1024
        ),
        cost_estimate=pl.CostEstimate(
            flops=6 * held * owners * tokens * full * ffe,
            bytes_accessed=6 * held * full * ffe,
            transcendentals=held * owners * tokens * ffe,
        ),
    )(
        queries,
        cache_keys.reshape(requests, cached, head_width),
        cache_values.reshape(requests, cached, head_width),
        new_keys.reshape(requests, head_width),
        new_values.reshape(requests, head_width),
        cache_lengths,
        moe_in,
        expert_ids.T,
        gate_index.T,
        gate_table.reshape(1, -1),
        jnp.swapaxes(gate_weight, 1, 2),
        jnp.swapaxes(up_weight, 1, 2),
        down_weight,
    )


def either(*args):
    moe_in, gate_weight = args[6], args[10]
    few_rows = lax.axis_size("afd") * moe_in.shape[0] <= 256
    if few_rows and lax.axis_size("tp") == 4 and gate_weight.shape[0] % GROUP == 0:
        return fused(*args)
    return on_device(*args)


def solution(mesh):
    placed = (
        P(("groups", "afd"), "tp", None),
        P(("groups", "afd"), "tp", None, None),
        P(("groups", "afd"), "tp", None, None),
        P(("groups", "afd"), "tp", None),
        P(("groups", "afd"), "tp", None),
        P(("groups", "afd")),
        P(("groups", "afd"), "tp"),
        P(("groups", "afd"), None),
        P(("groups", "afd"), None),
        P(),
        P("afd", None, "tp"),
        P("afd", None, "tp"),
        P("afd", "tp", None),
    )
    return jax.shard_map(
        either,
        mesh=mesh,
        in_specs=placed,
        out_specs=(P(("groups", "afd"), "tp", None), P(("groups", "afd"), "tp")),
        check_vma=False,
    )
```

```python
import functools
import math

import jax
import jax.numpy as jnp
from jax import lax
from jax.experimental import pallas as pl
from jax.experimental.pallas import tpu as pltpu
from jax.sharding import PartitionSpec as P

EXPERTS = 64
SLOTS = 2
GROUP = 4


def attend(queries, cache_keys, cache_values, new_keys, new_values, cache_lengths):
    requests, head_count, head_width = queries.shape
    kv_heads = cache_keys.shape[1]
    grouped = queries.reshape(requests, kv_heads, head_count // kv_heads, head_width)
    score_scale = 1.0 / math.sqrt(head_width)
    scores = (
        jnp.einsum("rkgd,rkld->rkgl", grouped, cache_keys, preferred_element_type=jnp.float32)
        * score_scale
    )
    fresh = (
        jnp.einsum("rkgd,rkd->rkg", grouped, new_keys, preferred_element_type=jnp.float32)
        * score_scale
    )
    positions = jnp.arange(cache_keys.shape[2], dtype=jnp.int32)
    valid = positions[None, None, None, :] < cache_lengths[:, None, None, None]
    masked = jnp.where(valid, scores, -jnp.inf)
    largest = jnp.maximum(jnp.max(masked, axis=3), fresh)
    exp_scores = jnp.where(valid, jnp.exp(masked - largest[..., None]), 0.0)
    fresh_prob = jnp.exp(fresh - largest)
    denominator = jnp.sum(exp_scores, axis=3) + fresh_prob
    weights = (exp_scores / denominator[..., None]).astype(jnp.bfloat16)
    fresh_weight = (fresh_prob / denominator).astype(jnp.bfloat16)
    mixed = jnp.einsum("rkgl,rkld->rkgd", weights, cache_values, preferred_element_type=jnp.float32)
    mixed = (
        mixed
        + fresh_weight.astype(jnp.float32)[..., None]
        * new_values.astype(jnp.float32)[:, :, None, :]
    )
    return mixed.reshape(requests, head_count, head_width).astype(jnp.bfloat16)


def on_device(
    queries,
    cache_keys,
    cache_values,
    new_keys,
    new_values,
    cache_lengths,
    moe_in,
    expert_ids,
    gate_index,
    gate_table,
    gate_weight,
    up_weight,
    down_weight,
):
    attn_out = attend(queries, cache_keys, cache_values, new_keys, new_values, cache_lengths)
    held_experts = gate_weight.shape[0]
    owner = lax.axis_index("afd")
    table_hits = (
        gate_index[..., None] == jnp.arange(gate_table.shape[0], dtype=jnp.int32)[None, None, :]
    ).astype(jnp.float32)
    raw_gates = jnp.sum(table_hits * gate_table[None, None, :], axis=2)
    route_weight = raw_gates / jnp.sum(raw_gates, axis=1, keepdims=True)
    chosen = expert_ids[..., None] == jnp.arange(EXPERTS, dtype=jnp.int32)
    routing = jnp.sum(jnp.where(chosen, route_weight[..., None], 0.0), axis=1)
    all_routing = lax.all_gather(routing, "afd", axis=0, tiled=True)
    held_routing = lax.dynamic_slice_in_dim(all_routing, owner * held_experts, held_experts, axis=1)
    all_rows = lax.all_gather(moe_in, "afd", axis=0, tiled=True)
    all_rows = lax.all_gather(all_rows, "tp", axis=1, tiled=True)
    gate_part = jnp.einsum("te,nef->tnf", all_rows, gate_weight, preferred_element_type=jnp.float32)
    up_part = jnp.einsum("te,nef->tnf", all_rows, up_weight, preferred_element_type=jnp.float32)
    hidden = jax.nn.silu(gate_part) * up_part
    scaled = (hidden * held_routing[:, :, None]).astype(jnp.bfloat16)
    partial_value = jnp.einsum("tnf,nfd->td", scaled, down_weight, preferred_element_type=jnp.float32)
    partial_value = partial_value.astype(jnp.bfloat16)
    summed = lax.psum_scatter(partial_value, "tp", scatter_dimension=1, tiled=True)
    moe_out = lax.psum_scatter(summed, "afd", scatter_dimension=0, tiled=True)
    return (attn_out, moe_out)


def fused_kernel(
    owners,
    queries_ref,
    keys_ref,
    values_ref,
    new_keys_ref,
    new_values_ref,
    lengths_ref,
    rows_ref,
    ids_ref,
    index_ref,
    table_ref,
    gate_hbm,
    up_hbm,
    down_hbm,
    attn_ref,
    moe_ref,
    gate_buf,
    up_buf,
    down_buf,
    all_rows,
    routing,
    hidden,
    part,
    core_got,
    x_got,
    z_got,
    gate_sem,
    up_sem,
    down_sem,
    zg_send,
    zg_recv,
    rt_send,
    rt_recv,
    xg_send,
    xg_recv,
    cg_send,
    cg_recv,
    cs_send,
    cs_recv,
    xs_send,
    xs_recv,
    zs_send,
    zs_recv,
):
    owner = lax.axis_index("afd")
    mine = lax.axis_index("tp")
    core_peer = mine + 1 - 2 * lax.rem(mine, 2)
    x_peer = lax.rem(mine + 2, 4)
    diagonal = lax.rem(core_peer + 2, 4)
    tokens, width = rows_ref.shape
    groups = gate_hbm.shape[0] // GROUP
    slots = gate_buf.shape[0]
    ffe = gate_hbm.shape[1]
    everyone = owners * tokens

    def group_copies(group, slot):
        experts = pl.ds(group * GROUP, GROUP)
        return (
            pltpu.make_async_copy(gate_hbm.at[experts], gate_buf.at[slot], gate_sem.at[slot]),
            pltpu.make_async_copy(up_hbm.at[experts], up_buf.at[slot], up_sem.at[slot]),
        )

    chunk_order = (diagonal, x_peer, core_peer, mine)

    def down_copy(step):
        columns = pl.ds(pl.multiple_of(chunk_order[step] * width, width), width)
        return pltpu.make_async_copy(
            down_hbm.at[:, :, columns], down_buf.at[step], down_sem.at[step]
        )

    def send(src, dst, send_sem, recv_sem, where):
        return pltpu.make_async_remote_copy(
            src_ref=src,
            dst_ref=dst,
            send_sem=send_sem,
            recv_sem=recv_sem,
            device_id=where,
            device_id_type=pl.DeviceIdType.MESH,
        )

    barrier = pltpu.get_barrier_semaphore()
    hops = sorted(range(1, owners), key=lambda j: min(j, owners - j))
    peers = [{"afd": lax.rem(owner + j, owners)} for j in hops]
    for where in peers + [{"tp": x_peer}, {"tp": core_peer}]:
        pl.semaphore_signal(barrier, inc=1, device_id=where, device_id_type=pl.DeviceIdType.MESH)

    for slot in range(slots):
        for copy in group_copies(slot, slot):
            copy.start()
    for step in range(4):
        down_copy(step).start()

    table = table_ref[...]
    places = lax.broadcasted_iota(jnp.int32, (tokens, table.shape[1]), 1)
    index = index_ref[...].T
    raw = [
        jnp.sum(jnp.where(places == index[:, k : k + 1], table, 0.0), axis=1, keepdims=True)
        for k in range(index.shape[1])
    ]
    total = sum(raw[1:], raw[0])
    lanes = lax.broadcasted_iota(jnp.int32, (tokens, 128), 1)
    ids = ids_ref[...].T
    placed = jnp.zeros((tokens, 128), jnp.float32)
    for k in range(index.shape[1]):
        placed = placed + jnp.where(lanes == ids[:, k : k + 1], raw[k] / total, 0.0)
    routing[owner] = placed
    all_rows[mine, owner] = rows_ref[...]

    pl.semaphore_wait(barrier, owners - 1 + 2)

    def z_gather(j, sender, target):
        return send(
            all_rows.at[mine, sender],
            all_rows.at[mine, sender],
            zg_send.at[j],
            zg_recv.at[j],
            {"afd": target},
        )

    def route_gather(j, sender, target):
        return send(
            routing.at[sender], routing.at[sender], rt_send.at[j], rt_recv.at[j], {"afd": target}
        )

    def x_gather(j, source):
        return send(
            all_rows.at[mine, source],
            all_rows.at[mine, source],
            xg_send.at[j],
            xg_recv.at[j],
            {"tp": x_peer},
        )

    def x_landed(j, source):
        return send(
            all_rows.at[x_peer, source],
            all_rows.at[x_peer, source],
            xg_send.at[j],
            xg_recv.at[j],
            {"tp": x_peer},
        )

    def core_gather(group, j, column, source):
        return send(
            all_rows.at[column, source],
            all_rows.at[column, source],
            cg_send.at[group, j],
            cg_recv.at[group, j],
            {"tp": core_peer},
        )

    for j in hops:
        target = lax.rem(owner + j, owners)
        z_gather(j, owner, target).start()
    x_gather(0, owner).start()
    core_gather(0, 0, mine, owner).start()
    for j in hops:
        route_gather(j, owner, lax.rem(owner + j, owners)).start()

    requests, heads, head_width = queries_ref.shape
    score_scale = 1.0 / math.sqrt(head_width)
    for r in range(requests):
        query = queries_ref[r]
        scores = (
            lax.dot_general(
                query, keys_ref[r], (((1,), (1,)), ((), ())), preferred_element_type=jnp.float32
            )
            * score_scale
        )
        new_key = new_keys_ref[pl.ds(r, 1), :].astype(jnp.float32)
        new_value = new_values_ref[pl.ds(r, 1), :].astype(jnp.float32)
        fresh = (
            jnp.sum(query.astype(jnp.float32) * new_key, axis=1, keepdims=True) * score_scale
        )
        positions = lax.broadcasted_iota(jnp.int32, scores.shape, 1)
        valid = positions < lengths_ref[r]
        masked = jnp.where(valid, scores, -jnp.inf)
        largest = jnp.maximum(jnp.max(masked, axis=1, keepdims=True), fresh)
        exp_scores = jnp.where(valid, jnp.exp(masked - largest), 0.0)
        fresh_prob = jnp.exp(fresh - largest)
        denominator = jnp.sum(exp_scores, axis=1, keepdims=True) + fresh_prob
        weights = (exp_scores / denominator).astype(jnp.bfloat16)
        fresh_weight = (fresh_prob / denominator).astype(jnp.bfloat16).astype(jnp.float32)
        mixed = jnp.dot(weights, values_ref[r], preferred_element_type=jnp.float32)
        attn_ref[r] = (mixed + fresh_weight * new_value).astype(jnp.bfloat16)

    order = [0] + hops
    for n, j in enumerate(order):
        source = lax.rem(owner + owners - j, owners)
        if j > 0:
            z_gather(j, source, source).wait_recv()
            x_gather(j, source).start()
            core_gather(0, j, mine, source).start()
        if n > 0:
            before = order[n - 1]
            source = lax.rem(owner + owners - before, owners)
            x_landed(before, source).wait_recv()
            core_gather(1, before, x_peer, source).start()
    last = order[-1]
    source = lax.rem(owner + owners - last, owners)
    x_landed(last, source).wait_recv()
    core_gather(1, last, x_peer, source).start()
    for j in order:
        source = lax.rem(owner + owners - j, owners)
        if j > 0:
            route_gather(j, source, source).wait_recv()
        core_gather(0, j, core_peer, source).wait_recv()
        core_gather(1, j, diagonal, source).wait_recv()
    gates = routing[...].reshape(everyone, 128)
    expert_lane = lax.broadcasted_iota(jnp.int32, (everyone, 128), 1)
    unit = lax.broadcasted_iota(jnp.int32, (everyone, GROUP * ffe), 1)

    def group_step(group, carry):
        slot = lax.rem(group, slots)
        for copy in group_copies(group, slot):
            copy.wait()

        def project(buf):
            return lax.dot_general(
                jnp.concatenate([all_rows[t].reshape(everyone, width) for t in range(4)], axis=1),
                buf[slot].reshape(GROUP * ffe, 4 * width),
                (((1,), (1,)), ((), ())),
                preferred_element_type=jnp.float32,
            )

        gate_part = project(gate_buf)
        up_part = project(up_buf)
        expert = GROUP * (owner * groups + group)
        scale = None
        for n in range(GROUP):
            column = jnp.sum(
                jnp.where(expert_lane == expert + n, gates, 0.0), axis=1, keepdims=True
            )
            scale = column if scale is None else jnp.where(unit < n * ffe, scale, column)
        value = gate_part / (1.0 + jnp.exp(-gate_part)) * up_part * scale
        hidden[group] = value.astype(jnp.bfloat16)

        @pl.when(group + slots < groups)
        def _():
            for copy in group_copies(group + slots, slot):
                copy.start()

        return carry

    lax.fori_loop(0, groups, group_step, 0)

    tile = 256

    def down_step(step):
        down_copy(step).wait()

        def tile_step(n, carry):
            columns = pl.ds(pl.multiple_of(n * tile, tile), tile)
            out = None
            for group in range(groups):
                right = down_buf[step, GROUP * group : GROUP * (group + 1), :, columns]
                term = jnp.dot(
                    hidden[group],
                    right.reshape(GROUP * ffe, tile),
                    preferred_element_type=jnp.float32,
                )
                out = term if out is None else out + term
            part[step, :, :, columns] = out.astype(jnp.bfloat16).reshape(owners, tokens, tile)
            return carry

        lax.fori_loop(0, width // tile, tile_step, 0)

    def core_send(k, step, j):
        piece = lax.rem(owner + j, owners)
        return send(
            part.at[step, piece],
            core_got.at[k, piece],
            cs_send.at[k, j],
            cs_recv.at[k, j],
            {"tp": core_peer},
        )

    def x_send(j, piece):
        return send(
            part.at[1, piece], x_got.at[piece], xs_send.at[j], xs_recv.at[j], {"tp": x_peer}
        )

    def z_send(j, piece):
        return send(
            part.at[3, piece], z_got.at[j], zs_send.at[j], zs_recv.at[j], {"afd": piece}
        )

    def add_in(step, piece, got):
        part[step, piece] = (
            part[step, piece].astype(jnp.float32) + got.astype(jnp.float32)
        ).astype(jnp.bfloat16)

    far_first = hops[::-1] + [0]
    down_step(0)
    for j in far_first:
        core_send(0, 0, j).start()
    down_step(1)
    for j in far_first:
        piece = lax.rem(owner + j, owners)
        core_send(0, 0, j).wait_recv()
        add_in(1, piece, core_got[0, piece])
        x_send(j, piece).start()
    down_step(2)
    for j in far_first:
        core_send(1, 2, j).start()
    down_step(3)
    for j in far_first:
        piece = lax.rem(owner + j, owners)
        core_send(1, 2, j).wait_recv()
        x_send(j, piece).wait_recv()
        part[3, piece] = (
            part[3, piece].astype(jnp.float32)
            + core_got[1, piece].astype(jnp.float32)
            + x_got[piece].astype(jnp.float32)
        ).astype(jnp.bfloat16)
        if j > 0:
            z_send(j, piece).start()
    result = part[3, owner].astype(jnp.float32)
    for j in hops:
        z_send(j, lax.rem(owner + j, owners)).wait_recv()
        result = result + z_got[j].astype(jnp.float32)
    moe_ref[...] = result.astype(jnp.bfloat16)
    for j in far_first:
        piece = lax.rem(owner + j, owners)
        core_send(0, 0, j).wait_send()
        core_send(1, 2, j).wait_send()
        x_send(j, piece).wait_send()
        if j > 0:
            z_send(j, piece).wait_send()
    for j in order:
        source = lax.rem(owner + owners - j, owners)
        if j > 0:
            z_gather(j, owner, source).wait_send()
            route_gather(j, owner, source).wait_send()
        x_gather(j, source).wait_send()
        core_gather(0, j, mine, source).wait_send()
        core_gather(1, j, x_peer, source).wait_send()


def fused(
    queries,
    cache_keys,
    cache_values,
    new_keys,
    new_values,
    cache_lengths,
    moe_in,
    expert_ids,
    gate_index,
    gate_table,
    gate_weight,
    up_weight,
    down_weight,
):
    owners = lax.axis_size("afd")
    tokens, width = moe_in.shape
    held, ffe, full = down_weight.shape
    requests, _, cached, head_width = cache_keys.shape
    vmem = pl.BlockSpec(memory_space=pltpu.VMEM)
    smem = pl.BlockSpec(memory_space=pltpu.SMEM)
    hbm = pl.BlockSpec(memory_space=pl.ANY)
    slots = min(SLOTS, held // GROUP)
    dma = pltpu.SemaphoreType.DMA
    bf16 = jnp.bfloat16
    return pl.pallas_call(
        functools.partial(fused_kernel, owners),
        out_shape=(
            jax.ShapeDtypeStruct(queries.shape, bf16),
            jax.ShapeDtypeStruct(moe_in.shape, bf16),
        ),
        in_specs=[vmem] * 5 + [smem] + [vmem] * 4 + [hbm] * 3,
        out_specs=(vmem, vmem),
        scratch_shapes=[
            pltpu.VMEM((slots, GROUP, ffe, full), bf16),
            pltpu.VMEM((slots, GROUP, ffe, full), bf16),
            pltpu.VMEM((4, held, ffe, width), bf16),
            pltpu.VMEM((4, owners, tokens, width), bf16),
            pltpu.VMEM((owners, tokens, 128), jnp.float32),
            pltpu.VMEM((held // GROUP, owners * tokens, GROUP * ffe), bf16),
            pltpu.VMEM((4, owners, tokens, width), bf16),
            pltpu.VMEM((2, owners, tokens, width), bf16),
            pltpu.VMEM((owners, tokens, width), bf16),
            pltpu.VMEM((owners, tokens, width), bf16),
            dma((slots,)),
            dma((slots,)),
            dma((4,)),
            dma((owners,)),
            dma((owners,)),
            dma((owners,)),
            dma((owners,)),
            dma((owners,)),
            dma((owners,)),
            dma((2, owners)),
            dma((2, owners)),
            dma((2, owners)),
            dma((2, owners)),
            dma((owners,)),
            dma((owners,)),
            dma((owners,)),
            dma((owners,)),
        ],
        compiler_params=pltpu.CompilerParams(
            collective_id=0, has_side_effects=True, vmem_limit_bytes=62 * 1024 * 1024
        ),
        cost_estimate=pl.CostEstimate(
            flops=6 * held * owners * tokens * full * ffe,
            bytes_accessed=6 * held * full * ffe,
            transcendentals=held * owners * tokens * ffe,
        ),
    )(
        queries,
        cache_keys.reshape(requests, cached, head_width),
        cache_values.reshape(requests, cached, head_width),
        new_keys.reshape(requests, head_width),
        new_values.reshape(requests, head_width),
        cache_lengths,
        moe_in,
        expert_ids.T,
        gate_index.T,
        gate_table.reshape(1, -1),
        jnp.swapaxes(gate_weight, 1, 2),
        jnp.swapaxes(up_weight, 1, 2),
        down_weight,
    )


def either(*args):
    moe_in, gate_weight = args[6], args[10]
    few_rows = lax.axis_size("afd") * moe_in.shape[0] <= 256
    if few_rows and lax.axis_size("tp") == 4 and gate_weight.shape[0] % GROUP == 0:
        return fused(*args)
    return on_device(*args)


def solution(mesh):
    placed = (
        P(("groups", "afd"), "tp", None),
        P(("groups", "afd"), "tp", None, None),
        P(("groups", "afd"), "tp", None, None),
        P(("groups", "afd"), "tp", None),
        P(("groups", "afd"), "tp", None),
        P(("groups", "afd")),
        P(("groups", "afd"), "tp"),
        P(("groups", "afd"), None),
        P(("groups", "afd"), None),
        P(),
        P("afd", None, "tp"),
        P("afd", None, "tp"),
        P("afd", "tp", None),
    )
    return jax.shard_map(
        either,
        mesh=mesh,
        in_specs=placed,
        out_specs=(P(("groups", "afd"), "tp", None), P(("groups", "afd"), "tp")),
        check_vma=False,
    )
```
